512 devices in a mesh: cfg: 2 (over y_lo), seq: 32 (over z, core), head: 8 (over y_hi, x).
Axes of the slice: x: 4, y: 4 (y_hi: 2, y_lo: 2; y = y_hi * 2 + y_lo), z: 16, core: 2. Of those that a mesh axis runs over, the one named last changes fastest.
Arguments:
- queries: bfloat16 [49152, 5120], P(('cfg', 'seq', 'head')), parts along dimension 0, may hold values from -90 to 90
- keys: bfloat16 [49152, 5120], P(('cfg', 'seq', 'head')), parts along dimension 0, may hold values from -4 to 4
- values: bfloat16 [49152, 5120], P(('cfg', 'seq', 'head')), parts along dimension 0, may hold values from -6 to 6
- windows: int32 [40, 3], replicated, may hold values from 0 to 1, as said below
Outputs:
- attended: bfloat16 [49152, 5120], P(('cfg', 'seq', 'head')), parts along dimension 0
The draws below stay inside these ranges and needn't reach their ends.
There are 2 independent parts, one for each index of `cfg`. The reference program is written for one: setup_inputs(seed, part) draws one part's arguments, and reference() takes and returns one part's arrays. A program takes and returns all parts, laid end to end along the dimension named above; an argument that names none is the same for every part. Nothing has to cross between parts.
Inputs may be any that keep to these rules, and one draw needn't show every extreme that they name: `windows`: each extent is 0 or 1; some head has all three extents 1 and another all three 0.
All inputs are finite; a program needn't handle non-finite values.
Results may differ from the reference program's by a relative error of at most 0.0046.
Values may be sent and summed in bfloat16 or wider, within the bound.
No kernel may reach another device: no remote copies, remote signals or barrier semaphores. Data moves between devices by JAX's collectives and lax.ppermute only.
A program may use at most 128 MiB of HBM per device.

```python
import jax
import jax.numpy as jnp
from jax import lax

HEADS = 40
HD = 128
TILE = 384
TH = 2
TW = 1
TOKENS = 24576


def key_rows(key):
    return jnp.clip(jax.random.normal(key, (TOKENS, HEADS * HD), jnp.float32), -4.0, 4.0)


def draw_keys(key, part):
    base = key_rows(key)
    return base.astype(jnp.bfloat16)


def draw_queries(key, part):
    key = jax.random.fold_in(key, 11)
    fresh = jnp.clip(jax.random.normal(key, (TOKENS, HEADS * HD), jnp.float32), -4.0, 4.0)
    return fresh.astype(jnp.bfloat16)


def draw_windows(key, part):
    key = jax.random.fold_in(key, 7)
    extents = jax.random.randint(jax.random.fold_in(key, 1), (HEADS, 3), 0, 2)
    widest = jax.random.randint(jax.random.fold_in(key, 2), (), 0, HEADS)
    narrow = (widest + 1 + jax.random.randint(jax.random.fold_in(key, 3), (), 0, HEADS - 1)) % HEADS
    heads = jnp.arange(HEADS, dtype=jnp.int32)[:, None]
    extents = jnp.where(heads == widest, 1, extents)
    extents = jnp.where(heads == narrow, 0, extents)
    return extents.astype(jnp.int32)


def block_levels(key, shape, pieces, low, high):
    level = 1.0
    for dim, blocks in pieces:
        draws = jax.random.uniform(jax.random.fold_in(jax.random.fold_in(key, 6), dim), (blocks,), jnp.float32, low / len(pieces), high / len(pieces))
        level = level * jnp.repeat(jnp.exp(draws), shape[dim] // blocks).reshape((-1,) + (1,) * (len(shape) - 1 - dim))
    return level


def gaussian(rng, shape, scale, bound, pieces=(), kind=jnp.bfloat16):
    values = scale * jax.random.normal(rng, shape, jnp.float32)
    if pieces:
        values = values * block_levels(rng, shape, pieces, -0.22, 0.18)
    return jnp.clip(values, -bound, bound).astype(kind)


def setup_inputs(seed: int = 0, part: int = 0) -> dict:
    key_of = jax.random.split(jax.random.key(seed), 5)
    own_keys = jax.random.split(jax.random.fold_in(key_of[4], part), 5)
    queries = draw_queries(jax.random.fold_in(jax.random.fold_in(key_of[4], part), 71), part)
    keys = draw_keys(jax.random.fold_in(jax.random.fold_in(key_of[4], part), 71), part)
    values = gaussian(own_keys[2], (TOKENS, HEADS * HD), 1.0, 6.0, ((0, 256),))
    windows = draw_windows(jax.random.fold_in(key_of[4], 71), part)
    return {"queries": queries, "keys": keys, "values": values, "windows": windows}


def reference(queries, keys, values, windows):
    lrows = TILE * TH * TW
    nlayers = TOKENS // lrows
    scale = HD ** -0.5
    blank = jnp.zeros((lrows, HEADS * HD), jnp.bfloat16)
    key_pad = jnp.concatenate([blank, keys, blank], axis=0)
    value_pad = jnp.concatenate([blank, values, blank], axis=0)
    q_tile = jnp.arange(lrows, dtype=jnp.int32) // TILE
    k_index = jnp.arange(3 * lrows, dtype=jnp.int32)
    k_tile = (k_index % lrows) // TILE
    k_layer = k_index // lrows - 1
    row_gap = jnp.abs(q_tile[:, None] // TW - k_tile[None, :] // TW)
    col_gap = jnp.abs(q_tile[:, None] % TW - k_tile[None, :] % TW)
    lay_gap = jnp.abs(k_layer)

    def one_layer(layer):
        start = (layer * lrows).astype(jnp.int32)
        qblock = lax.dynamic_slice_in_dim(queries, start, lrows, 0).reshape(lrows, HEADS, HD)
        kblock = lax.dynamic_slice_in_dim(key_pad, start, 3 * lrows, 0).reshape(3 * lrows, HEADS, HD)
        vblock = lax.dynamic_slice_in_dim(value_pad, start, 3 * lrows, 0).reshape(3 * lrows, HEADS, HD)
        scores = jnp.einsum("qhd,khd->hqk", qblock.astype(jnp.float32), kblock.astype(jnp.float32)) * scale
        inside = (layer + k_layer >= 0) & (layer + k_layer < nlayers)
        visible = (lay_gap[None, None, :] <= windows[:, 0, None, None]) & (row_gap[None] <= windows[:, 1, None, None]) & (col_gap[None] <= windows[:, 2, None, None]) & inside[None, None, :]
        scores = jnp.where(visible, scores, -jnp.inf)
        largest = jnp.max(scores, axis=-1, keepdims=True)
        weights = jnp.exp(scores - largest)
        total = jnp.sum(weights, axis=-1)
        probs = weights.astype(jnp.bfloat16)
        mixed = jnp.einsum("hqk,khd->qhd", probs.astype(jnp.float32), vblock.astype(jnp.float32))
        mixed = mixed / jnp.transpose(total)[:, :, None]
        return mixed.astype(jnp.bfloat16).reshape(lrows, HEADS * HD)

    blocks = lax.map(one_layer, jnp.arange(nlayers, dtype=jnp.int32))
    return blocks.reshape(TOKENS, HEADS * HD)
```

```python
import functools
import math

import jax
import jax.numpy as jnp
from jax import lax
from jax.experimental import pallas as pl
from jax.experimental.pallas import tpu as pltpu
from jax.sharding import PartitionSpec as P

HD = 128
TILE = 384
ROWS = 2
NEAR = 3
TURNS = (6, 5, 7, 4, 2, 1, 3, 0)
ANY = pl.BlockSpec(memory_space=pl.ANY)
SMEM = pl.BlockSpec(memory_space=pltpu.SMEM)
VMEM = pl.BlockSpec(memory_space=pltpu.VMEM)


def column(index):
    return pl.ds(pl.multiple_of(index * HD, HD), HD)


def rank_of(device, slot, count):
    return slot * count + (device if slot % 2 == 0 else count - 1 - device)


def sort_heads(windows, order):
    heads = order.shape[0]

    def kind(head):
        return 3 - 2 * windows[0, head] - windows[1, head]

    def tally(head, counts):
        this = kind(head)
        return tuple(n + (this == i).astype(jnp.int32) for i, n in enumerate(counts))

    zero = jnp.int32(0)
    counts = lax.fori_loop(0, heads, tally, (zero,) * 4)
    starts = (zero, counts[0], counts[0] + counts[1], counts[0] + counts[1] + counts[2])

    def place(head, nexts):
        this = kind(head)
        spot = zero
        for i, n in enumerate(nexts):
            spot = jnp.where(this == i, n, spot)
        order[spot] = head
        return tuple(n + (this == i).astype(jnp.int32) for i, n in enumerate(nexts))

    lax.fori_loop(0, heads, place, starts)


def fetch(arrays, held, sems):
    copies = [
        pltpu.make_async_copy(array, held.at[i], sems.at[i]) for i, array in enumerate(arrays)
    ]
    for copy in copies:
        copy.start()
    return copies


def fill(order, device, devices, held, parts, room):
    at = 0
    for i, slots in parts:
        for slot in slots:
            head = order[rank_of(device, slot, devices)]
            room[at] = held[i, :, column(head)]
            at += 1


def pack_first(near, windows, keys, values, *refs):
    *packed, order, held, room, in_sems, out_sems = refs
    arrivals = fetch((keys, values), held, in_sems)
    sort_heads(windows, order)
    for copy in arrivals:
        copy.wait()
    copies = []
    for turn in TURNS:
        device = lax.axis_index("head") ^ turn
        fill(order, device, len(packed), held, ((0, near), (1, near)), room.at[turn])
        copy = pltpu.make_async_copy(room.at[turn], packed[turn], out_sems.at[turn])
        copy.start()
        copies.append(copy)
    for copy in copies:
        copy.wait()


def pack_second(slots, far, order, queries, keys, values, packed, held, room, in_sems, out_sems):
    arrivals = fetch((queries, keys, values), held, in_sems)
    for copy in arrivals:
        copy.wait()
    copies = []
    devices = packed.shape[0]
    for device in range(devices):
        fill(order, device, devices, held, ((0, slots), (1, far), (2, far)), room.at[device])
        copy = pltpu.make_async_copy(room.at[device], packed.at[device], out_sems.at[device])
        copy.start()
        copies.append(copy)
    for copy in copies:
        copy.wait()


def call_pack(body, scalar, arrays, devices, blocks, out_shape, out_specs, name):
    tokens, model = arrays[0].shape
    return pl.pallas_call(
        body,
        out_shape=out_shape,
        in_specs=[SMEM] + [ANY] * len(arrays),
        out_specs=out_specs,
        scratch_shapes=[
            pltpu.VMEM((len(arrays), tokens, model), jnp.bfloat16),
            pltpu.VMEM((devices, blocks, tokens, HD), jnp.bfloat16),
            pltpu.SemaphoreType.DMA((len(arrays),)),
            pltpu.SemaphoreType.DMA((devices,)),
        ],
        compiler_params=pltpu.CompilerParams(vmem_limit_bytes=16 * 2**20),
        cost_estimate=pl.CostEstimate(
            flops=0, bytes_accessed=4 * devices * blocks * tokens * HD, transcendentals=0
        ),
        name=name,
    )(scalar, *arrays)


def gather(after, *refs):
    *chunks, out, sems = refs
    copies = [
        pltpu.make_async_copy(chunk, out.at[lax.axis_index("head") ^ turn], sems.at[turn])
        for turn, chunk in enumerate(chunks)
    ]
    for copy in copies:
        copy.start()
    for copy in copies:
        copy.wait()


def call_gather(after, chunks, name):
    devices = len(chunks)
    return pl.pallas_call(
        gather,
        out_shape=jax.ShapeDtypeStruct((devices, *chunks[0].shape), chunks[0].dtype),
        in_specs=[ANY] * (devices + 1),
        out_specs=VMEM,
        scratch_shapes=[pltpu.SemaphoreType.DMA((devices,))],
        cost_estimate=pl.CostEstimate(
            flops=0, bytes_accessed=4 * devices * chunks[0].size, transcendentals=0
        ),
        name=name,
    )(after, *chunks)


def unpack(split, order, first, second, out):
    devices = first.shape[0]
    slots = first.shape[1] + second.shape[1]
    for device in range(devices):
        for slot in range(slots):
            array, at = (first, slot) if slot < split else (second, slot - split)
            head = order[rank_of(device, slot, devices)]
            out[:, column(head)] = array[device, at]


def attend(slots, at, has_rim, devices, *refs):
    if has_rim:
        order, windows, queries, own, before, after, out, q, k, v, sems = refs
    else:
        order, windows, queries, own, out, q, k, v, sems = refs
    count = len(slots)
    group, tokens = q.shape[1:3]
    q_at, k_at, v_at = at
    layer, device, layers = lax.axis_index("seq"), lax.axis_index("head"), lax.axis_size("seq")

    def extents(n):
        slot = slots[0] + n
        back = jnp.where(slot % 2 == 0, device, devices - 1 - device)
        head = order[slot * devices + back]
        return windows[0, head], windows[1, head]

    def pair(array, n, part, k_col, v_col):
        chunks = pl.ds(part * group, group)
        return (
            pltpu.make_async_copy(array.at[:, k_col + n], k.at[n, chunks], sems.at[n, 1 + 2 * part]),
            pltpu.make_async_copy(
                array.at[:, v_col + n], v.at[n, chunks, :, pl.ds(0, HD)], sems.at[n, 2 + 2 * part]
            ),
        )

    def own_copies(n):
        mid = 1 if has_rim else 0
        query = pltpu.make_async_copy(queries.at[:, q_at + n], q.at[n], sems.at[n, 0])
        return (query, *pair(own, n, mid, k_at, v_at))

    def near_sides(n):
        far_sight, _ = extents(n)
        return (
            ((far_sight > 0) & (layer > 0), pair(before, n, 0, 0, count)),
            ((far_sight > 0) & (layer < layers - 1), pair(after, n, 2, 0, count)),
        )

    def issue(n, carry):
        for copy in own_copies(n):
            copy.start()
        if has_rim:
            for wanted, copies in near_sides(n):

                @pl.when(wanted)
                def _():
                    for copy in copies:
                        copy.start()

        return carry

    def arrive(n):
        for copy in own_copies(n):
            copy.wait()
        if has_rim:
            for wanted, copies in near_sides(n):

                @pl.when(wanted)
                def _():
                    for copy in copies:
                        copy.wait()

    lax.fori_loop(0, count, issue, 0)
    v[..., HD:] = jnp.ones((*v.shape[:3], HD), v.dtype)
    factor = HD ** (-0.5) * math.log2(math.e)

    def block(n, tile, first, parts, both):
        keep = group if both else group // ROWS
        shift = 0 if both else tile * (group // ROWS)
        spans = [pl.ds((first + part) * group + shift, keep) for part in range(parts)]
        some = group // ROWS // 2
        pieces = [pl.ds(tile * (group // ROWS) + piece * some, some) for piece in range(2)]
        scores = [
            [
                lax.dot_general(
                    q[n, chunks].reshape(some * tokens, HD),
                    k[n, s].reshape(keep * tokens, HD),
                    (((1,), (1,)), ((), ())),
                    preferred_element_type=jnp.float32,
                )
                for s in spans
            ]
            for chunks in pieces
        ]
        for chunks, row in zip(pieces, scores):
            largest = functools.reduce(
                jnp.maximum, [jnp.max(score, axis=1, keepdims=True) for score in row]
            )
            mixed = None
            for s, score in zip(spans, row):
                probs = jnp.exp2((score - largest) * factor).astype(jnp.bfloat16)
                value = v[n, s].reshape(keep * tokens, 2 * HD)
                term = jnp.dot(probs, value, preferred_element_type=jnp.float32)
                mixed = term if mixed is None else mixed + term
            result = mixed[:, :HD] / mixed[:, HD:]
            out[chunks, n] = result.astype(out.dtype).reshape(some, tokens, HD)

    def each(n, carry):
        arrive(n)
        far_sight, both_rows = extents(n)
        if has_rim:
            first = jnp.where(far_sight > 0, jnp.where(layer > 0, 0, 1), 1)
            last = jnp.where(far_sight > 0, jnp.where(layer < layers - 1, 2, 1), 1)
        else:
            first = last = jnp.int32(0)
        parts = last - first + 1
        for both in (False, True):
            for number in (1, 2, 3) if has_rim else (1,):

                @pl.when((parts == number) & ((both_rows > 0) == both))
                def _():
                    def tiles(tile, inner):
                        block(n, tile, first, number, both)
                        return inner

                    lax.fori_loop(0, ROWS, tiles, 0)

        return carry

    lax.fori_loop(0, count, each, 0)


def call_attend(slots, at, order, windows, queries, own, sides, name):
    count = len(slots)
    devices, _, tokens, _ = own.shape
    span = devices * tokens
    parts = 1 + len(sides)
    pairs = count * span * span * parts
    return pl.pallas_call(
        functools.partial(attend, slots, at, bool(sides), devices),
        out_shape=jax.ShapeDtypeStruct((devices, count, tokens, HD), jnp.bfloat16),
        in_specs=[SMEM] * 2 + [ANY] * (2 + len(sides)),
        out_specs=pl.BlockSpec(memory_space=pltpu.VMEM),
        scratch_shapes=[
            pltpu.VMEM((count, devices, tokens, HD), jnp.bfloat16),
            pltpu.VMEM((count, parts * devices, tokens, HD), jnp.bfloat16),
            pltpu.VMEM((count, parts * devices, tokens, 2 * HD), jnp.bfloat16),
            pltpu.SemaphoreType.DMA((count, 7)),
        ],
        compiler_params=pltpu.CompilerParams(vmem_limit_bytes=48 * 2**20),
        cost_estimate=pl.CostEstimate(
            flops=2 * pairs * HD, bytes_accessed=8 * count * span * HD, transcendentals=pairs
        ),
        name=name,
    )(order, windows, queries, own, *sides)


def shards(queries, keys, values, windows):
    tokens, model = queries.shape
    heads = model // HD
    devices = lax.axis_size("head")
    layers = lax.axis_size("seq")
    slots = heads // devices
    near, far = tuple(range(NEAR)), tuple(range(NEAR, slots))
    windows = windows.T
    def moved(number):
        return pl.CostEstimate(
            flops=0, bytes_accessed=4 * number * tokens * HD, transcendentals=0
        )

    def swap(array):
        return lax.all_to_all(array, "head", split_axis=0, concat_axis=0, tiled=True)

    first_blocks, blocks = 2 * len(near), slots + 2 * len(far)
    chunk = jax.ShapeDtypeStruct((first_blocks, tokens, HD), jnp.bfloat16)
    *first, order = call_pack(
        functools.partial(pack_first, near), windows, (keys, values), devices, first_blocks,
        (chunk,) * devices + (jax.ShapeDtypeStruct((heads,), jnp.int32),),
        (ANY,) * devices + (SMEM,), "pack_near_keys_values",
    )
    chunks = list(first)
    for turn in TURNS[:-1]:
        chunks[turn] = lax.ppermute(first[turn], "head", [(i, i ^ turn) for i in range(devices)])
    second = call_pack(
        functools.partial(pack_second, tuple(range(slots)), far), order, (queries, keys, values),
        devices, blocks, jax.ShapeDtypeStruct((devices, blocks, tokens, HD), jnp.bfloat16), ANY,
        "pack_queries_and_rest",
    )
    rest = swap(second)
    near_kv = call_gather(second, chunks, "gather_near_keys_values")

    def neighbours(array):
        ends = layers - 1
        return (
            lax.ppermute(array, "seq", [(i, i + 1) for i in range(ends)]),
            lax.ppermute(array, "seq", [(i + 1, i) for i in range(ends)]),
        )

    sides = neighbours(near_kv)

    def with_far():
        far_sides = neighbours(rest[:, slots:])
        return call_attend(
            far, (NEAR, slots, slots + len(far)), order, windows, rest, rest, far_sides,
            "attend_far_slots_three_layers",
        )

    def without_far():
        return call_attend(
            far, (NEAR, slots, slots + len(far)), order, windows, rest, rest, (),
            "attend_far_slots_own_layer",
        )

    wide = jnp.sum(windows[0]) > NEAR * devices
    far_out = lax.cond(wide, with_far, without_far)
    far_back = swap(far_out)
    near_out = call_attend(
        near, (0, 0, NEAR), order, windows, rest, near_kv, sides, "attend_near_slots"
    )
    near_back = swap(near_out)

    number = slots * devices
    return pl.pallas_call(
        functools.partial(unpack, NEAR),
        out_shape=jax.ShapeDtypeStruct((tokens, model), jnp.bfloat16),
        in_specs=[SMEM, VMEM, VMEM],
        out_specs=VMEM,
        cost_estimate=moved(number),
        name="unpack_attended",
    )(order, near_back, far_back)


def solution(mesh):
    placed = P(("cfg", "seq", "head"), None)
    return jax.shard_map(
        shards,
        mesh=mesh,
        in_specs=(placed, placed, placed, P()),
        out_specs=placed,
        check_vma=False,
    )
```

```python
import functools
import math

import jax
import jax.numpy as jnp
from jax import lax
from jax.experimental import pallas as pl
from jax.experimental.pallas import tpu as pltpu
from jax.sharding import PartitionSpec as P

HD = 128
TILE = 384
ROWS = 2
NEAR = 3
ANY = pl.BlockSpec(memory_space=pl.ANY)
SMEM = pl.BlockSpec(memory_space=pltpu.SMEM)
VMEM = pl.BlockSpec(memory_space=pltpu.VMEM)


def column(index):
    return pl.ds(pl.multiple_of(index * HD, HD), HD)


def rank_of(device, slot, count):
    return slot * count + (device if slot % 2 == 0 else count - 1 - device)


def sort_heads(windows, order):
    heads = order.shape[0]

    def kind(head):
        return 3 - 2 * windows[0, head] - windows[1, head]

    def tally(head, counts):
        this = kind(head)
        return tuple(n + (this == i).astype(jnp.int32) for i, n in enumerate(counts))

    zero = jnp.int32(0)
    counts = lax.fori_loop(0, heads, tally, (zero,) * 4)
    starts = (zero, counts[0], counts[0] + counts[1], counts[0] + counts[1] + counts[2])

    def place(head, nexts):
        this = kind(head)
        spot = zero
        for i, n in enumerate(nexts):
            spot = jnp.where(this == i, n, spot)
        order[spot] = head
        return tuple(n + (this == i).astype(jnp.int32) for i, n in enumerate(nexts))

    lax.fori_loop(0, heads, place, starts)


def pack(order, parts, packed):
    devices = packed.shape[0]
    for device in range(devices):
        at = 0
        for array, slots in parts:
            for slot in slots:
                head = order[rank_of(device, slot, devices)]
                packed[device, at] = array[:, column(head)]
                at += 1


def pack_first(near, windows, keys, values, packed, order):
    sort_heads(windows, order)
    pack(order, ((keys, near), (values, near)), packed)


def pack_second(slots, far, order, queries, keys, values, packed):
    pack(order, ((queries, slots), (keys, far), (values, far)), packed)


def unpack(order, blocks, out):
    devices, slots = blocks.shape[:2]
    for device in range(devices):
        for slot in range(slots):
            head = order[rank_of(device, slot, devices)]
            out[:, column(head)] = blocks[device, slot]


def attend(near, slots, wide, order, windows, rest, near_kv, *refs):
    *sides, out, q, k, v, sems = refs
    devices, tokens = q.shape[1:3]
    far = slots - near
    layer, device, layers = lax.axis_index("seq"), lax.axis_index("head"), lax.axis_size("seq")

    def extents(n):
        back = jnp.where(n % 2 == 0, device, devices - 1 - device)
        head = order[n * devices + back]
        return windows[0, head], windows[1, head]

    def pair(n, part, array, k_at, v_at):
        chunks = pl.ds(part * devices, devices)
        return (
            pltpu.make_async_copy(array.at[:, k_at], k.at[n, chunks], sems.at[n, 1 + 2 * part]),
            pltpu.make_async_copy(
                array.at[:, v_at], v.at[n, chunks, :, pl.ds(0, HD)], sems.at[n, 2 + 2 * part]
            ),
        )

    def own_copies(n):
        query = pltpu.make_async_copy(rest.at[:, n], q.at[n], sems.at[n, 0])
        if n < near:
            return (query, *pair(n, 1, near_kv, n, near + n))
        return (query, *pair(n, 1, rest, slots + n - near, slots + far + n - near))

    def side_copies(n):
        sight, _ = extents(n)
        if n < near:
            arrays, k_at, v_at = sides[:2], n, near + n
        elif wide:
            arrays, k_at, v_at = sides[2:], n - near, far + n - near
        else:
            return ()
        return (
            ((sight > 0) & (layer > 0), pair(n, 0, arrays[0], k_at, v_at)),
            ((sight > 0) & (layer < layers - 1), pair(n, 2, arrays[1], k_at, v_at)),
        )

    def each_copy(n, act):
        for copy in own_copies(n):
            act(copy)
        for wanted, copies in side_copies(n):

            @pl.when(wanted)
            def _():
                for copy in copies:
                    act(copy)

    for n in range(slots):
        each_copy(n, lambda copy: copy.start())
    v[..., HD:] = jnp.ones((*v.shape[:3], HD), v.dtype)
    factor = HD ** (-0.5) * math.log2(math.e)

    def block(n, tile, first, parts, both):
        half = devices // ROWS
        keep = devices if both else half
        shift = 0 if both else tile * half
        spans = [pl.ds((first + part) * devices + shift, keep) for part in range(parts)]
        query = q[n, pl.ds(tile * half, half)].reshape(half * tokens, HD)
        scores = [
            lax.dot_general(
                query,
                k[n, s].reshape(keep * tokens, HD),
                (((1,), (1,)), ((), ())),
                preferred_element_type=jnp.float32,
            )
            for s in spans
        ]
        largest = functools.reduce(
            jnp.maximum, [jnp.max(score, axis=1, keepdims=True) for score in scores]
        )
        mixed = None
        for s, score in zip(spans, scores):
            probs = jnp.exp2((score - largest) * factor).astype(jnp.bfloat16)
            value = v[n, s].reshape(keep * tokens, 2 * HD)
            term = jnp.dot(probs, value, preferred_element_type=jnp.float32)
            mixed = term if mixed is None else mixed + term
        result = mixed[:, :HD] / mixed[:, HD:]
        out[pl.ds(tile * half, half), n] = result.astype(out.dtype).reshape(half, tokens, HD)

    def each(n, carry):
        for i in range(slots):

            @pl.when(n == i)
            def _():
                each_copy(i, lambda copy: copy.wait())

        sight, rows = extents(n)
        first = jnp.where((sight > 0) & (layer > 0), 0, 1)
        last = jnp.where((sight > 0) & (layer < layers - 1), 2, 1)
        parts = last - first + 1
        for both in (False, True):
            for number in (1, 2, 3):

                @pl.when((parts == number) & ((rows > 0) == both))
                def _():
                    def tiles(tile, inner):
                        block(n, tile, first, number, both)
                        return inner

                    lax.fori_loop(0, ROWS, tiles, 0)

        return carry

    lax.fori_loop(0, slots, each, 0)


def call_attend(near, slots, order, windows, rest, near_kv, sides, name):
    devices, _, tokens, _ = rest.shape
    span = devices * tokens
    pairs = slots * span * span * 2
    return pl.pallas_call(
        functools.partial(attend, near, slots, len(sides) > 2),
        out_shape=jax.ShapeDtypeStruct((devices, slots, tokens, HD), jnp.bfloat16),
        in_specs=[SMEM] * 2 + [ANY] * (2 + len(sides)),
        out_specs=VMEM,
        scratch_shapes=[
            pltpu.VMEM((slots, devices, tokens, HD), jnp.bfloat16),
            pltpu.VMEM((slots, 3 * devices, tokens, HD), jnp.bfloat16),
            pltpu.VMEM((slots, 3 * devices, tokens, 2 * HD), jnp.bfloat16),
            pltpu.SemaphoreType.DMA((slots, 7)),
        ],
        compiler_params=pltpu.CompilerParams(vmem_limit_bytes=48 * 2**20),
        cost_estimate=pl.CostEstimate(
            flops=4 * pairs * HD, bytes_accessed=16 * slots * span * HD, transcendentals=pairs
        ),
        name=name,
    )(order, windows, rest, near_kv, *sides)


def shards(queries, keys, values, windows):
    tokens, model = queries.shape
    heads = model // HD
    devices = lax.axis_size("head")
    layers = lax.axis_size("seq")
    slots = heads // devices
    near, far = tuple(range(NEAR)), tuple(range(NEAR, slots))
    windows = windows.T

    def packed(blocks):
        return jax.ShapeDtypeStruct((devices, blocks, tokens, HD), jnp.bfloat16)

    def moved(blocks):
        return pl.CostEstimate(
            flops=0, bytes_accessed=4 * devices * blocks * tokens * HD, transcendentals=0
        )

    def swap(array):
        return lax.all_to_all(array, "head", split_axis=0, concat_axis=0, tiled=True)

    def neighbours(array):
        ends = layers - 1
        return (
            lax.ppermute(array, "seq", [(i, i + 1) for i in range(ends)]),
            lax.ppermute(array, "seq", [(i + 1, i) for i in range(ends)]),
        )

    blocks = 2 * len(near)
    first, order = pl.pallas_call(
        functools.partial(pack_first, near),
        out_shape=(packed(blocks), jax.ShapeDtypeStruct((heads,), jnp.int32)),
        in_specs=[SMEM, VMEM, VMEM],
        out_specs=(VMEM, SMEM),
        cost_estimate=moved(blocks),
        name="pack_near_keys_values",
    )(windows, keys, values)
    near_kv = swap(first)

    blocks = slots + 2 * len(far)
    second = pl.pallas_call(
        functools.partial(pack_second, tuple(range(slots)), far),
        out_shape=packed(blocks),
        in_specs=[SMEM, VMEM, VMEM, VMEM],
        out_specs=VMEM,
        cost_estimate=moved(blocks),
        name="pack_queries_and_rest",
    )(order, queries, keys, values)
    sides = neighbours(near_kv)
    rest = swap(second)

    def with_far():
        return call_attend(
            NEAR, slots, order, windows, rest, near_kv, (*sides, *neighbours(rest[:, slots:])),
            "attend_all_slots_wide",
        )

    def without_far():
        return call_attend(
            NEAR, slots, order, windows, rest, near_kv, sides, "attend_near_slots_wide"
        )

    wide = jnp.sum(windows[0]) > NEAR * devices
    attended = swap(lax.cond(wide, with_far, without_far))

    return pl.pallas_call(
        unpack,
        out_shape=jax.ShapeDtypeStruct((tokens, model), jnp.bfloat16),
        in_specs=[SMEM, VMEM],
        out_specs=VMEM,
        cost_estimate=moved(slots),
        name="unpack_attended",
    )(order, attended)


def solution(mesh):
    placed = P(("cfg", "seq", "head"), None)
    return jax.shard_map(
        shards,
        mesh=mesh,
        in_specs=(placed, placed, placed, P()),
        out_specs=placed,
        check_vma=False,
    )
```

```python
import functools
import math

import jax
import jax.numpy as jnp
from jax import lax
from jax.experimental import pallas as pl
from jax.experimental.pallas import tpu as pltpu
from jax.sharding import PartitionSpec as P

HD = 128
TILE = 384
ROWS = 2
PIECES = 2
NEAR = 3
ANY = pl.BlockSpec(memory_space=pl.ANY)
SMEM = pl.BlockSpec(memory_space=pltpu.SMEM)
VMEM = pl.BlockSpec(memory_space=pltpu.VMEM)


def column(index):
    return pl.ds(pl.multiple_of(index * HD, HD), HD)


def rank_of(device, slot, count):
    return slot * count + (device if slot % 2 == 0 else count - 1 - device)


def sort_heads(windows, order):
    heads = order.shape[0]

    def kind(head):
        return 3 - 2 * windows[0, head] - windows[1, head]

    def tally(head, counts):
        this = kind(head)
        return tuple(n + (this == i).astype(jnp.int32) for i, n in enumerate(counts))

    zero = jnp.int32(0)
    counts = lax.fori_loop(0, heads, tally, (zero,) * 4)
    starts = (zero, counts[0], counts[0] + counts[1], counts[0] + counts[1] + counts[2])

    def place(head, nexts):
        this = kind(head)
        spot = zero
        for i, n in enumerate(nexts):
            spot = jnp.where(this == i, n, spot)
        order[spot] = head
        return tuple(n + (this == i).astype(jnp.int32) for i, n in enumerate(nexts))

    lax.fori_loop(0, heads, place, starts)


def pack(order, parts, packed):
    devices = packed.shape[0]
    for device in range(devices):
        at = 0
        for array, slots in parts:
            for slot in slots:
                head = order[rank_of(device, slot, devices)]
                packed[device, at] = array[:, column(head)]
                at += 1


def pack_first(near, windows, keys, values, packed, order):
    sort_heads(windows, order)
    pack(order, ((keys, near), (values, near)), packed)


def pack_second(slots, far, order, queries, keys, values, packed):
    pack(order, ((queries, slots), (keys, far), (values, far)), packed)


def unpack(order, blocks, out):
    devices, slots = blocks.shape[:2]
    for device in range(devices):
        for slot in range(slots):
            head = order[rank_of(device, slot, devices)]
            out[:, column(head)] = blocks[device, slot]


def attend(near, slots, wide, order, windows, rest, near_kv, *refs):
    *sides, out, q, k, v, sems = refs
    devices, tokens = q.shape[1:3]
    far = slots - near
    layer, device, layers = lax.axis_index("seq"), lax.axis_index("head"), lax.axis_size("seq")

    def extents(n):
        back = jnp.where(n % 2 == 0, device, devices - 1 - device)
        head = order[n * devices + back]
        return windows[0, head], windows[1, head]

    def pair(n, part, array, k_at, v_at):
        chunks = pl.ds(part * devices, devices)
        return (
            pltpu.make_async_copy(array.at[:, k_at], k.at[n, chunks], sems.at[n, 1 + 2 * part]),
            pltpu.make_async_copy(
                array.at[:, v_at], v.at[n, chunks, :, pl.ds(0, HD)], sems.at[n, 2 + 2 * part]
            ),
        )

    def own_copies(n):
        query = pltpu.make_async_copy(rest.at[:, n], q.at[n], sems.at[n, 0])
        if n < near:
            return (query, *pair(n, 1, near_kv, n, near + n))
        return (query, *pair(n, 1, rest, slots + n - near, slots + far + n - near))

    def side_copies(n):
        sight, _ = extents(n)
        if n < near:
            arrays, k_at, v_at = sides[:2], n, near + n
        elif wide:
            arrays, k_at, v_at = sides[2:], n - near, far + n - near
        else:
            return ()
        return (
            ((sight > 0) & (layer > 0), pair(n, 0, arrays[0], k_at, v_at)),
            ((sight > 0) & (layer < layers - 1), pair(n, 2, arrays[1], k_at, v_at)),
        )

    def each_copy(n, act):
        for copy in own_copies(n):
            act(copy)
        for wanted, copies in side_copies(n):

            @pl.when(wanted)
            def _():
                for copy in copies:
                    act(copy)

    for n in reversed(range(slots)):
        each_copy(n, lambda copy: copy.start())
    v[..., HD:] = jnp.ones((*v.shape[:3], HD), v.dtype)
    factor = HD ** (-0.5) * math.log2(math.e)

    half = devices // ROWS
    some = half // PIECES

    def score(n, piece, spans):
        query = q[n, pl.ds(piece * some, some)].reshape(some * tokens, HD)
        return [
            lax.dot_general(
                query,
                k[n, s].reshape(s.size * tokens, HD),
                (((1,), (1,)), ((), ())),
                preferred_element_type=jnp.float32,
            )
            for s in spans
        ]

    def finish(n, piece, spans, scores):
        lanes = [score[:, i : i + HD] for score in scores for i in range(0, score.shape[1], HD)]
        largest = jnp.max(functools.reduce(jnp.maximum, lanes), axis=1, keepdims=True)
        mixed = None
        for s, score in zip(spans, scores):
            probs = jnp.exp2((score - largest) * factor).astype(jnp.bfloat16)
            value = v[n, s].reshape(s.size * tokens, 2 * HD)
            term = jnp.dot(probs, value, preferred_element_type=jnp.float32)
            mixed = term if mixed is None else mixed + term
        result = mixed[:, :HD] / mixed[:, HD:]
        out[pl.ds(piece * some, some), n] = result.astype(out.dtype).reshape(some, tokens, HD)

    def block(n, pieces, first, parts, both):
        def spans(piece):
            keep = devices if both else half
            shift = 0 if both else piece // PIECES * half
            return [pl.ds((first + part) * devices + shift, keep) for part in range(parts)]

        ahead = score(n, pieces[0], spans(pieces[0]))
        for this, after in zip(pieces, [*pieces[1:], None]):
            now = ahead
            if after is not None:
                ahead = score(n, after, spans(after))
            finish(n, this, spans(this), now)

    def each(step, carry):
        n = slots - 1 - step
        for i in range(slots):

            @pl.when(n == i)
            def _():
                each_copy(i, lambda copy: copy.wait())

        sight, rows = extents(n)
        first = jnp.where((sight > 0) & (layer > 0), 0, 1)
        last = jnp.where((sight > 0) & (layer < layers - 1), 2, 1)
        parts = last - first + 1
        for both in (False, True):
            for number in (1, 2, 3):

                @pl.when((parts == number) & ((rows > 0) == both))
                def _():
                    if number == 1:
                        block(n, list(range(ROWS * PIECES)), first, number, both)
                        return

                    def tiles(tile, inner):
                        pieces = [tile * PIECES + i for i in range(PIECES)]
                        block(n, pieces, first, number, both)
                        return inner

                    lax.fori_loop(0, ROWS, tiles, 0)

        return carry

    lax.fori_loop(0, slots, each, 0)


def call_attend(near, slots, order, windows, rest, near_kv, sides, name):
    devices, _, tokens, _ = rest.shape
    span = devices * tokens
    pairs = slots * span * span * 2
    return pl.pallas_call(
        functools.partial(attend, near, slots, len(sides) > 2),
        out_shape=jax.ShapeDtypeStruct((devices, slots, tokens, HD), jnp.bfloat16),
        in_specs=[SMEM] * 2 + [ANY] * (2 + len(sides)),
        out_specs=VMEM,
        scratch_shapes=[
            pltpu.VMEM((slots, devices, tokens, HD), jnp.bfloat16),
            pltpu.VMEM((slots, 3 * devices, tokens, HD), jnp.bfloat16),
            pltpu.VMEM((slots, 3 * devices, tokens, 2 * HD), jnp.bfloat16),
            pltpu.SemaphoreType.DMA((slots, 7)),
        ],
        compiler_params=pltpu.CompilerParams(vmem_limit_bytes=48 * 2**20),
        cost_estimate=pl.CostEstimate(
            flops=4 * pairs * HD, bytes_accessed=16 * slots * span * HD, transcendentals=pairs
        ),
        name=name,
    )(order, windows, rest, near_kv, *sides)


def shards(queries, keys, values, windows):
    tokens, model = queries.shape
    heads = model // HD
    devices = lax.axis_size("head")
    layers = lax.axis_size("seq")
    slots = heads // devices
    near, far = tuple(range(NEAR)), tuple(range(NEAR, slots))
    windows = windows.T

    def packed(blocks):
        return jax.ShapeDtypeStruct((devices, blocks, tokens, HD), jnp.bfloat16)

    def moved(blocks):
        return pl.CostEstimate(
            flops=0, bytes_accessed=4 * devices * blocks * tokens * HD, transcendentals=0
        )

    def swap(array):
        return lax.all_to_all(array, "head", split_axis=0, concat_axis=0, tiled=True)

    def neighbours(array):
        ends = layers - 1
        return (
            lax.ppermute(array, "seq", [(i, i + 1) for i in range(ends)]),
            lax.ppermute(array, "seq", [(i + 1, i) for i in range(ends)]),
        )

    blocks = 2 * len(near)
    first, order = pl.pallas_call(
        functools.partial(pack_first, near),
        out_shape=(packed(blocks), jax.ShapeDtypeStruct((heads,), jnp.int32)),
        in_specs=[SMEM, VMEM, VMEM],
        out_specs=(VMEM, SMEM),
        cost_estimate=moved(blocks),
        name="pack_near_keys_values",
    )(windows, keys, values)
    near_kv = swap(first)

    blocks = slots + 2 * len(far)
    second = pl.pallas_call(
        functools.partial(pack_second, tuple(range(slots)), far),
        out_shape=packed(blocks),
        in_specs=[SMEM, VMEM, VMEM, VMEM],
        out_specs=VMEM,
        cost_estimate=moved(blocks),
        name="pack_queries_and_rest",
    )(order, queries, keys, values)
    sides = neighbours(near_kv)
    rest = swap(second)

    def with_far():
        return call_attend(
            NEAR, slots, order, windows, rest, near_kv, (*sides, *neighbours(rest[:, slots:])),
            "attend_all_slots_wide",
        )

    def without_far():
        return call_attend(
            NEAR, slots, order, windows, rest, near_kv, sides, "attend_near_slots_wide"
        )

    wide = jnp.sum(windows[0]) > NEAR * devices
    attended = swap(lax.cond(wide, with_far, without_far))

    return pl.pallas_call(
        unpack,
        out_shape=jax.ShapeDtypeStruct((tokens, model), jnp.bfloat16),
        in_specs=[SMEM, VMEM],
        out_specs=VMEM,
        cost_estimate=moved(slots),
        name="unpack_attended",
    )(order, attended)


def solution(mesh):
    placed = P(("cfg", "seq", "head"), None)
    return jax.shard_map(
        shards,
        mesh=mesh,
        in_specs=(placed, placed, placed, P()),
        out_specs=placed,
        check_vma=False,
    )
```

```python
import functools
import math

import jax
import jax.numpy as jnp
from jax import lax
from jax.experimental import pallas as pl
from jax.experimental.pallas import tpu as pltpu
from jax.sharding import PartitionSpec as P

HD = 128
TILE = 384
ROWS = 2
PIECES = 2
NEAR = 3
ANY = pl.BlockSpec(memory_space=pl.ANY)
SMEM = pl.BlockSpec(memory_space=pltpu.SMEM)
VMEM = pl.BlockSpec(memory_space=pltpu.VMEM)


def column(index):
    return pl.ds(pl.multiple_of(index * HD, HD), HD)


def rank_of(device, slot, count):
    return slot * count + (device if slot % 2 == 0 else count - 1 - device)


def sort_heads(windows, order):
    heads = order.shape[0]

    def kind(head):
        return 3 - 2 * windows[0, head] - windows[1, head]

    def tally(head, counts):
        this = kind(head)
        return tuple(n + (this == i).astype(jnp.int32) for i, n in enumerate(counts))

    zero = jnp.int32(0)
    counts = lax.fori_loop(0, heads, tally, (zero,) * 4)
    starts = (zero, counts[0], counts[0] + counts[1], counts[0] + counts[1] + counts[2])

    def place(head, nexts):
        this = kind(head)
        spot = zero
        for i, n in enumerate(nexts):
            spot = jnp.where(this == i, n, spot)
        order[spot] = head
        return tuple(n + (this == i).astype(jnp.int32) for i, n in enumerate(nexts))

    lax.fori_loop(0, heads, place, starts)


def pack(order, parts, packed):
    devices = packed.shape[0]
    for device in range(devices):
        at = 0
        for array, slots in parts:
            for slot in slots:
                head = order[rank_of(device, slot, devices)]
                packed[device, at] = array[:, column(head)]
                at += 1


def pack_first(near, windows, keys, values, packed, order):
    @pl.when(pl.program_id(0) == 0)
    def _():
        sort_heads(windows, order)

    pack(order, ((keys, near), (values, near)), packed)


def pack_second(slots, far, order, queries, keys, values, packed):
    pack(order, ((queries, slots), (keys, far), (values, far)), packed)


def unpack(order, first, second, out):
    devices = first.shape[0]
    for device in range(devices):
        at = 0
        for array in (first, second):
            for block in range(array.shape[1]):
                head = order[rank_of(device, at, devices)]
                out[:, column(head)] = array[device, block]
                at += 1


def attend(slots, at, order, windows, queries, own, *refs):
    *sides, out, q, k, v, sems = refs
    q_at, own_at = at
    has_sides = bool(sides)
    count, (devices, tokens) = len(slots), q.shape[1:3]
    mid = 1 if has_sides else 0
    layer, device, layers = lax.axis_index("seq"), lax.axis_index("head"), lax.axis_size("seq")

    def extents(n):
        slot = slots[0] + n
        back = jnp.where(slot % 2 == 0, device, devices - 1 - device)
        head = order[slot * devices + back]
        return windows[0, head], windows[1, head]

    def pair(n, part, array, k_at, v_at):
        chunks = pl.ds(part * devices, devices)
        return (
            pltpu.make_async_copy(array.at[:, k_at], k.at[n, chunks], sems.at[n, 1 + 2 * part]),
            pltpu.make_async_copy(
                array.at[:, v_at], v.at[n, chunks, :, pl.ds(0, HD)], sems.at[n, 2 + 2 * part]
            ),
        )

    def own_copies(n):
        query = pltpu.make_async_copy(queries.at[:, q_at + n], q.at[n], sems.at[n, 0])
        return (query, *pair(n, mid, own, own_at + n, own_at + count + n))

    def side_copies(n):
        if not has_sides:
            return ()
        sight, _ = extents(n)
        return (
            ((sight > 0) & (layer > 0), pair(n, 0, sides[0], n, count + n)),
            ((sight > 0) & (layer < layers - 1), pair(n, 2, sides[1], n, count + n)),
        )

    def each_copy(n, act):
        for copy in own_copies(n):
            act(copy)
        for wanted, copies in side_copies(n):

            @pl.when(wanted)
            def _():
                for copy in copies:
                    act(copy)

    for n in reversed(range(count)):
        each_copy(n, lambda copy: copy.start())
    v[..., HD:] = jnp.ones((*v.shape[:3], HD), v.dtype)
    factor = HD ** (-0.5) * math.log2(math.e)

    half = devices // ROWS
    some = half // PIECES

    def score(n, piece, spans):
        query = q[n, pl.ds(piece * some, some)].reshape(some * tokens, HD)
        return [
            lax.dot_general(
                query,
                k[n, s].reshape(s.size * tokens, HD),
                (((1,), (1,)), ((), ())),
                preferred_element_type=jnp.float32,
            )
            for s in spans
        ]

    def finish(n, piece, spans, scores):
        lanes = [score[:, i : i + HD] for score in scores for i in range(0, score.shape[1], HD)]
        largest = jnp.max(functools.reduce(jnp.maximum, lanes), axis=1, keepdims=True)
        mixed = None
        for s, score in zip(spans, scores):
            probs = jnp.exp2((score - largest) * factor).astype(jnp.bfloat16)
            value = v[n, s].reshape(s.size * tokens, 2 * HD)
            term = jnp.dot(probs, value, preferred_element_type=jnp.float32)
            mixed = term if mixed is None else mixed + term
        result = mixed[:, :HD] / mixed[:, HD:]
        out[pl.ds(piece * some, some), n] = result.astype(out.dtype).reshape(some, tokens, HD)

    def block(n, pieces, first, parts, both):
        def spans(piece):
            keep = devices if both else half
            shift = 0 if both else piece // PIECES * half
            return [pl.ds((first + part) * devices + shift, keep) for part in range(parts)]

        ahead = score(n, pieces[0], spans(pieces[0]))
        for this, after in zip(pieces, [*pieces[1:], None]):
            now = ahead
            if after is not None:
                ahead = score(n, after, spans(after))
            finish(n, this, spans(this), now)

    def each(step, carry):
        n = count - 1 - step
        for i in range(count):

            @pl.when(n == i)
            def _():
                each_copy(i, lambda copy: copy.wait())

        sight, rows = extents(n)
        first, last = mid, mid
        if has_sides:
            first = jnp.where((sight > 0) & (layer > 0), 0, 1)
            last = jnp.where((sight > 0) & (layer < layers - 1), 2, 1)
        parts = last - first + 1
        for both in (False, True):
            for number in (1, 2, 3) if has_sides else (1,):

                @pl.when((parts == number) & ((rows > 0) == both))
                def _():
                    if number == 1:
                        block(n, list(range(ROWS * PIECES)), first, number, both)
                        return

                    def tiles(tile, inner):
                        pieces = [tile * PIECES + i for i in range(PIECES)]
                        block(n, pieces, first, number, both)
                        return inner

                    lax.fori_loop(0, ROWS, tiles, 0)

        return carry

    lax.fori_loop(0, count, each, 0)


def call_attend(slots, at, order, windows, queries, own, sides, name):
    devices, _, tokens, _ = own.shape
    count, span = len(slots), devices * tokens
    layers = 3 if sides else 1
    pairs = count * span * span * layers
    return pl.pallas_call(
        functools.partial(attend, slots, at),
        out_shape=jax.ShapeDtypeStruct((devices, count, tokens, HD), jnp.bfloat16),
        in_specs=[SMEM] * 2 + [ANY] * (2 + len(sides)),
        out_specs=VMEM,
        scratch_shapes=[
            pltpu.VMEM((count, devices, tokens, HD), jnp.bfloat16),
            pltpu.VMEM((count, layers * devices, tokens, HD), jnp.bfloat16),
            pltpu.VMEM((count, layers * devices, tokens, 2 * HD), jnp.bfloat16),
            pltpu.SemaphoreType.DMA((count, 7)),
        ],
        compiler_params=pltpu.CompilerParams(vmem_limit_bytes=48 * 2**20),
        cost_estimate=pl.CostEstimate(
            flops=4 * pairs * HD, bytes_accessed=16 * count * span * HD, transcendentals=pairs
        ),
        name=name,
    )(order, windows, queries, own, *sides)


def shards(queries, keys, values, windows):
    tokens, model = queries.shape
    heads = model // HD
    devices = lax.axis_size("head")
    layers = lax.axis_size("seq")
    slots = heads // devices
    near, far = tuple(range(NEAR)), tuple(range(NEAR, slots))
    windows = windows.T
    steps = 2 if tokens % 32 == 0 else 1
    some = tokens // steps
    rows = pl.BlockSpec((some, model), lambda i: (i, 0))

    def blocks_of(count):
        return pl.BlockSpec((devices, count, some, HD), lambda i: (0, 0, i, 0))

    def packed(count):
        return jax.ShapeDtypeStruct((devices, count, tokens, HD), jnp.bfloat16)

    def moved(count):
        return pl.CostEstimate(
            flops=0, bytes_accessed=4 * devices * count * tokens * HD, transcendentals=0
        )

    def swap(array):
        return lax.all_to_all(array, "head", split_axis=0, concat_axis=0, tiled=True)

    def neighbours(array):
        ends = layers - 1
        return (
            lax.ppermute(array, "seq", [(i, i + 1) for i in range(ends)]),
            lax.ppermute(array, "seq", [(i + 1, i) for i in range(ends)]),
        )

    blocks = 2 * len(near)
    first, order = pl.pallas_call(
        functools.partial(pack_first, near),
        grid=(steps,),
        out_shape=(packed(blocks), jax.ShapeDtypeStruct((heads,), jnp.int32)),
        in_specs=[SMEM, rows, rows],
        out_specs=(blocks_of(blocks), SMEM),
        cost_estimate=moved(blocks),
        name="pack_near_keys_values",
    )(windows, keys, values)
    near_kv = swap(first)

    blocks = slots + 2 * len(far)
    second = pl.pallas_call(
        functools.partial(pack_second, tuple(range(slots)), far),
        grid=(steps,),
        out_shape=packed(blocks),
        in_specs=[SMEM, rows, rows, rows],
        out_specs=blocks_of(blocks),
        cost_estimate=moved(blocks),
        name="pack_queries_and_rest",
    )(order, queries, keys, values)
    sides = neighbours(near_kv)
    rest = swap(second)

    def with_sides():
        far_sides = neighbours(rest[:, slots:])
        return call_attend(
            far, (NEAR, slots), order, windows, rest, rest, far_sides,
            "attend_far_slots_three_layers",
        )

    def own_layer():
        return call_attend(
            far, (NEAR, slots), order, windows, rest, rest, (), "attend_far_slots_own_layer"
        )

    wide = jnp.sum(windows[0]) > NEAR * devices
    far_back = swap(lax.cond(wide, with_sides, own_layer))
    near_back = swap(
        call_attend(near, (0, 0), order, windows, rest, near_kv, sides, "attend_near_slots")
    )

    return pl.pallas_call(
        unpack,
        grid=(steps,),
        out_shape=jax.ShapeDtypeStruct((tokens, model), jnp.bfloat16),
        in_specs=[SMEM, blocks_of(len(near)), blocks_of(len(far))],
        out_specs=rows,
        cost_estimate=moved(slots),
        name="unpack_attended",
    )(order, near_back, far_back)


def solution(mesh):
    placed = P(("cfg", "seq", "head"), None)
    return jax.shard_map(
        shards,
        mesh=mesh,
        in_specs=(placed, placed, placed, P()),
        out_specs=placed,
        check_vma=False,
    )
```

```python
import functools
import math

import jax
import jax.numpy as jnp
from jax import lax
from jax.experimental import pallas as pl
from jax.experimental.pallas import tpu as pltpu
from jax.sharding import PartitionSpec as P

HD = 128
TILE = 384
ROWS = 2
PIECES = 2
NEAR = 3
ANY = pl.BlockSpec(memory_space=pl.ANY)
SMEM = pl.BlockSpec(memory_space=pltpu.SMEM)
VMEM = pl.BlockSpec(memory_space=pltpu.VMEM)


def column(index):
    return pl.ds(pl.multiple_of(index * HD, HD), HD)


def rank_of(device, slot, count):
    return slot * count + (device if slot % 2 == 0 else count - 1 - device)


def sort_heads(windows, order):
    heads = order.shape[0]

    def kind(head):
        return 3 - 2 * windows[0, head] - windows[1, head]

    def tally(head, counts):
        this = kind(head)
        return tuple(n + (this == i).astype(jnp.int32) for i, n in enumerate(counts))

    zero = jnp.int32(0)
    counts = lax.fori_loop(0, heads, tally, (zero,) * 4)
    starts = (zero, counts[0], counts[0] + counts[1], counts[0] + counts[1] + counts[2])

    def place(head, nexts):
        this = kind(head)
        spot = zero
        for i, n in enumerate(nexts):
            spot = jnp.where(this == i, n, spot)
        order[spot] = head
        return tuple(n + (this == i).astype(jnp.int32) for i, n in enumerate(nexts))

    lax.fori_loop(0, heads, place, starts)


def pack(order, parts, packed):
    devices = packed.shape[0]
    for device in range(devices):
        at = 0
        for array, slots in parts:
            for slot in slots:
                head = order[rank_of(device, slot, devices)]
                packed[device, at] = array[:, column(head)]
                at += 1


def pack_first(near, windows, keys, values, packed, order):
    @pl.when(pl.program_id(0) == 0)
    def _():
        sort_heads(windows, order)

    pack(order, ((keys, near), (values, near)), packed)


def pack_second(slots, far, order, queries, keys, values, packed):
    pack(order, ((queries, slots), (keys, far), (values, far)), packed)


def unpack(order, blocks, out):
    devices, slots = blocks.shape[:2]
    for device in range(devices):
        for slot in range(slots):
            head = order[rank_of(device, slot, devices)]
            out[:, column(head)] = blocks[device, slot]


def attend(near, slots, wide, order, windows, rest, near_kv, *refs):
    *sides, out, q, k, v, sems = refs
    devices, tokens = q.shape[1:3]
    far = slots - near
    layer, device, layers = lax.axis_index("seq"), lax.axis_index("head"), lax.axis_size("seq")

    def extents(n):
        back = jnp.where(n % 2 == 0, device, devices - 1 - device)
        head = order[n * devices + back]
        return windows[0, head], windows[1, head]

    def pair(n, part, array, k_at, v_at):
        chunks = pl.ds(part * devices, devices)
        return (
            pltpu.make_async_copy(array.at[:, k_at], k.at[n, chunks], sems.at[n, 1 + 2 * part]),
            pltpu.make_async_copy(
                array.at[:, v_at], v.at[n, chunks, :, pl.ds(0, HD)], sems.at[n, 2 + 2 * part]
            ),
        )

    def own_copies(n):
        query = pltpu.make_async_copy(rest.at[:, n], q.at[n], sems.at[n, 0])
        if n < near:
            return (query, *pair(n, 1, near_kv, n, near + n))
        return (query, *pair(n, 1, rest, slots + n - near, slots + far + n - near))

    def side_copies(n):
        sight, _ = extents(n)
        if n < near:
            arrays, k_at, v_at = sides[:2], n, near + n
        elif wide:
            arrays, k_at, v_at = sides[2:], n - near, far + n - near
        else:
            return ()
        return (
            ((sight > 0) & (layer > 0), pair(n, 0, arrays[0], k_at, v_at)),
            ((sight > 0) & (layer < layers - 1), pair(n, 2, arrays[1], k_at, v_at)),
        )

    def each_copy(n, act):
        for copy in own_copies(n):
            act(copy)
        for wanted, copies in side_copies(n):

            @pl.when(wanted)
            def _():
                for copy in copies:
                    act(copy)

    for n in reversed(range(slots)):
        each_copy(n, lambda copy: copy.start())
    v[..., HD:] = jnp.ones((*v.shape[:3], HD), v.dtype)
    factor = HD ** (-0.5) * math.log2(math.e)

    half = devices // ROWS
    some = half // PIECES

    def score(n, piece, spans):
        query = q[n, pl.ds(piece * some, some)].reshape(some * tokens, HD)
        return [
            lax.dot_general(
                query,
                k[n, s].reshape(s.size * tokens, HD),
                (((1,), (1,)), ((), ())),
                preferred_element_type=jnp.float32,
            )
            for s in spans
        ]

    def finish(n, piece, spans, scores):
        lanes = [score[:, i : i + HD] for score in scores for i in range(0, score.shape[1], HD)]
        largest = jnp.max(functools.reduce(jnp.maximum, lanes), axis=1, keepdims=True)
        mixed = None
        for s, score in zip(spans, scores):
            probs = jnp.exp2((score - largest) * factor).astype(jnp.bfloat16)
            value = v[n, s].reshape(s.size * tokens, 2 * HD)
            term = jnp.dot(probs, value, preferred_element_type=jnp.float32)
            mixed = term if mixed is None else mixed + term
        result = mixed[:, :HD] / mixed[:, HD:]
        out[pl.ds(piece * some, some), n] = result.astype(out.dtype).reshape(some, tokens, HD)

    def block(n, pieces, first, parts, both):
        def spans(piece):
            keep = devices if both else half
            shift = 0 if both else piece // PIECES * half
            return [pl.ds((first + part) * devices + shift, keep) for part in range(parts)]

        ahead = score(n, pieces[0], spans(pieces[0]))
        for this, after in zip(pieces, [*pieces[1:], None]):
            now = ahead
            if after is not None:
                ahead = score(n, after, spans(after))
            finish(n, this, spans(this), now)

    def each(step, carry):
        n = slots - 1 - step
        for i in range(slots):

            @pl.when(n == i)
            def _():
                each_copy(i, lambda copy: copy.wait())

        sight, rows = extents(n)
        first = jnp.where((sight > 0) & (layer > 0), 0, 1)
        last = jnp.where((sight > 0) & (layer < layers - 1), 2, 1)
        parts = last - first + 1
        for both in (False, True):
            for number in (1, 2, 3):

                @pl.when((parts == number) & ((rows > 0) == both))
                def _():
                    if number == 1:
                        block(n, list(range(ROWS * PIECES)), first, number, both)
                        return

                    def tiles(tile, inner):
                        pieces = [tile * PIECES + i for i in range(PIECES)]
                        block(n, pieces, first, number, both)
                        return inner

                    lax.fori_loop(0, ROWS, tiles, 0)

        return carry

    lax.fori_loop(0, slots, each, 0)


def call_attend(near, slots, order, windows, rest, near_kv, sides, name):
    devices, _, tokens, _ = rest.shape
    span = devices * tokens
    pairs = slots * span * span * 2
    return pl.pallas_call(
        functools.partial(attend, near, slots, len(sides) > 2),
        out_shape=jax.ShapeDtypeStruct((devices, slots, tokens, HD), jnp.bfloat16),
        in_specs=[SMEM] * 2 + [ANY] * (2 + len(sides)),
        out_specs=VMEM,
        scratch_shapes=[
            pltpu.VMEM((slots, devices, tokens, HD), jnp.bfloat16),
            pltpu.VMEM((slots, 3 * devices, tokens, HD), jnp.bfloat16),
            pltpu.VMEM((slots, 3 * devices, tokens, 2 * HD), jnp.bfloat16),
            pltpu.SemaphoreType.DMA((slots, 7)),
        ],
        compiler_params=pltpu.CompilerParams(vmem_limit_bytes=48 * 2**20),
        cost_estimate=pl.CostEstimate(
            flops=4 * pairs * HD, bytes_accessed=16 * slots * span * HD, transcendentals=pairs
        ),
        name=name,
    )(order, windows, rest, near_kv, *sides)


def shards(queries, keys, values, windows):
    tokens, model = queries.shape
    heads = model // HD
    devices = lax.axis_size("head")
    layers = lax.axis_size("seq")
    slots = heads // devices
    near, far = tuple(range(NEAR)), tuple(range(NEAR, slots))
    windows = windows.T
    steps = 2 if tokens % 32 == 0 else 1
    some = tokens // steps
    rows = pl.BlockSpec((some, model), lambda i: (i, 0))

    def blocks_of(count):
        return pl.BlockSpec((devices, count, some, HD), lambda i: (0, 0, i, 0))

    def packed(blocks):
        return jax.ShapeDtypeStruct((devices, blocks, tokens, HD), jnp.bfloat16)

    def moved(blocks):
        return pl.CostEstimate(
            flops=0, bytes_accessed=4 * devices * blocks * tokens * HD, transcendentals=0
        )

    def swap(array):
        return lax.all_to_all(array, "head", split_axis=0, concat_axis=0, tiled=True)

    def neighbours(array):
        ends = layers - 1
        return (
            lax.ppermute(array, "seq", [(i, i + 1) for i in range(ends)]),
            lax.ppermute(array, "seq", [(i + 1, i) for i in range(ends)]),
        )

    blocks = 2 * len(near)
    first, order = pl.pallas_call(
        functools.partial(pack_first, near),
        grid=(steps,),
        out_shape=(packed(blocks), jax.ShapeDtypeStruct((heads,), jnp.int32)),
        in_specs=[SMEM, rows, rows],
        out_specs=(blocks_of(blocks), SMEM),
        cost_estimate=moved(blocks),
        name="pack_near_keys_values",
    )(windows, keys, values)
    near_kv = swap(first)

    blocks = slots + 2 * len(far)
    second = pl.pallas_call(
        functools.partial(pack_second, tuple(range(slots)), far),
        grid=(steps,),
        out_shape=packed(blocks),
        in_specs=[SMEM, rows, rows, rows],
        out_specs=blocks_of(blocks),
        cost_estimate=moved(blocks),
        name="pack_queries_and_rest",
    )(order, queries, keys, values)
    sides = neighbours(near_kv)
    rest = swap(second)

    def with_far():
        return call_attend(
            NEAR, slots, order, windows, rest, near_kv, (*sides, *neighbours(rest[:, slots:])),
            "attend_all_slots_wide",
        )

    def without_far():
        return call_attend(
            NEAR, slots, order, windows, rest, near_kv, sides, "attend_near_slots_wide"
        )

    wide = jnp.sum(windows[0]) > NEAR * devices
    attended = swap(lax.cond(wide, with_far, without_far))

    return pl.pallas_call(
        unpack,
        grid=(steps,),
        out_shape=jax.ShapeDtypeStruct((tokens, model), jnp.bfloat16),
        in_specs=[SMEM, blocks_of(slots)],
        out_specs=rows,
        cost_estimate=moved(slots),
        name="unpack_attended",
    )(order, attended)


def solution(mesh):
    placed = P(("cfg", "seq", "head"), None)
    return jax.shard_map(
        shards,
        mesh=mesh,
        in_specs=(placed, placed, placed, P()),
        out_specs=placed,
        check_vma=False,
    )
```

```python
import functools
import math

import jax
import jax.numpy as jnp
from jax import lax
from jax.experimental import pallas as pl
from jax.experimental.pallas import tpu as pltpu
from jax.sharding import PartitionSpec as P

HD = 128
TILE = 384
ROWS = 2
PIECES = 2
NEAR = 3
ANY = pl.BlockSpec(memory_space=pl.ANY)
SMEM = pl.BlockSpec(memory_space=pltpu.SMEM)
VMEM = pl.BlockSpec(memory_space=pltpu.VMEM)


def column(index):
    return pl.ds(pl.multiple_of(index * HD, HD), HD)


def rank_of(device, slot, count):
    return slot * count + (device if slot % 2 == 0 else count - 1 - device)


def sort_heads(windows, order):
    heads = order.shape[0]

    def kind(head):
        return 3 - 2 * windows[0, head] - windows[1, head]

    def tally(head, counts):
        this = kind(head)
        return tuple(n + (this == i).astype(jnp.int32) for i, n in enumerate(counts))

    zero = jnp.int32(0)
    counts = lax.fori_loop(0, heads, tally, (zero,) * 4)
    starts = (zero, counts[0], counts[0] + counts[1], counts[0] + counts[1] + counts[2])

    def place(head, nexts):
        this = kind(head)
        spot = zero
        for i, n in enumerate(nexts):
            spot = jnp.where(this == i, n, spot)
        order[spot] = head
        return tuple(n + (this == i).astype(jnp.int32) for i, n in enumerate(nexts))

    lax.fori_loop(0, heads, place, starts)


def pack(order, parts, packed):
    devices = packed.shape[0]
    for device in range(devices):
        at = 0
        for array, slots in parts:
            for slot in slots:
                head = order[rank_of(device, slot, devices)]
                packed[device, at] = array[:, column(head)]
                at += 1


def pack_first(near, windows, keys, values, packed, order):
    @pl.when(pl.program_id(0) == 0)
    def _():
        sort_heads(windows, order)

    pack(order, ((keys, near), (values, near)), packed)


def pack_second(slots, far, order, queries, keys, values, packed):
    pack(order, ((queries, slots), (keys, far), (values, far)), packed)


def unpack(order, blocks, out):
    devices, slots = blocks.shape[:2]
    for device in range(devices):
        for slot in range(slots):
            head = order[rank_of(device, slot, devices)]
            out[:, column(head)] = blocks[device, slot]


def attend(near, slots, wide, order, windows, rest, near_kv, *refs):
    *sides, out, q, k, v, sems = refs
    devices, tokens = q.shape[1:3]
    far = slots - near
    layer, device, layers = lax.axis_index("seq"), lax.axis_index("head"), lax.axis_size("seq")

    def extents(n):
        back = jnp.where(n % 2 == 0, device, devices - 1 - device)
        head = order[n * devices + back]
        return windows[0, head], windows[1, head]

    def pair(n, part, array, k_at, v_at):
        chunks = pl.ds(part * devices, devices)
        return (
            pltpu.make_async_copy(array.at[:, k_at], k.at[n, chunks], sems.at[n, 1 + 2 * part]),
            pltpu.make_async_copy(
                array.at[:, v_at], v.at[n, chunks, :, pl.ds(0, HD)], sems.at[n, 2 + 2 * part]
            ),
        )

    def own_copies(n):
        query = pltpu.make_async_copy(rest.at[:, n], q.at[n], sems.at[n, 0])
        if n < near:
            return (query, *pair(n, 1, near_kv, n, near + n))
        return (query, *pair(n, 1, rest, slots + n - near, slots + far + n - near))

    def side_copies(n):
        sight, _ = extents(n)
        if n < near:
            arrays, k_at, v_at = sides[:2], n, near + n
        elif wide:
            arrays, k_at, v_at = sides[2:], n - near, far + n - near
        else:
            return ()
        return (
            ((sight > 0) & (layer > 0), pair(n, 0, arrays[0], k_at, v_at)),
            ((sight > 0) & (layer < layers - 1), pair(n, 2, arrays[1], k_at, v_at)),
        )

    def each_copy(n, act):
        for copy in own_copies(n):
            act(copy)
        for wanted, copies in side_copies(n):

            @pl.when(wanted)
            def _():
                for copy in copies:
                    act(copy)

    for n in reversed(range(slots)):
        each_copy(n, lambda copy: copy.start())
    v[..., HD:] = jnp.ones((*v.shape[:3], HD), v.dtype)
    factor = HD ** (-0.5) * math.log2(math.e)

    half = devices // ROWS
    some = half // PIECES

    def score(n, piece, spans):
        query = q[n, pl.ds(piece * some, some)].reshape(some * tokens, HD)
        return [
            lax.dot_general(
                query,
                k[n, s].reshape(s.size * tokens, HD),
                (((1,), (1,)), ((), ())),
                preferred_element_type=jnp.float32,
            )
            for s in spans
        ]

    def finish(n, piece, spans, scores):
        lanes = [score[:, i : i + HD] for score in scores for i in range(0, score.shape[1], HD)]
        largest = jnp.max(functools.reduce(jnp.maximum, lanes), axis=1, keepdims=True)
        mixed = None
        for s, score in zip(spans, scores):
            probs = jnp.exp2((score - largest) * factor).astype(jnp.bfloat16)
            value = v[n, s].reshape(s.size * tokens, 2 * HD)
            term = jnp.dot(probs, value, preferred_element_type=jnp.float32)
            mixed = term if mixed is None else mixed + term
        result = mixed[:, :HD] / mixed[:, HD:]
        out[pl.ds(piece * some, some), n] = result.astype(out.dtype).reshape(some, tokens, HD)

    def block(n, pieces, first, parts, both):
        def spans(piece):
            keep = devices if both else half
            shift = 0 if both else piece // PIECES * half
            return [pl.ds((first + part) * devices + shift, keep) for part in range(parts)]

        ahead = score(n, pieces[0], spans(pieces[0]))
        for this, after in zip(pieces, [*pieces[1:], None]):
            now = ahead
            if after is not None:
                ahead = score(n, after, spans(after))
            finish(n, this, spans(this), now)

    def each(step, carry):
        n = slots - 1 - step
        for i in range(slots):

            @pl.when(n == i)
            def _():
                each_copy(i, lambda copy: copy.wait())

        sight, rows = extents(n)
        first = jnp.where((sight > 0) & (layer > 0), 0, 1)
        last = jnp.where((sight > 0) & (layer < layers - 1), 2, 1)
        parts = last - first + 1
        for both in (False, True):
            for number in (1, 2, 3):

                @pl.when((parts == number) & ((rows > 0) == both))
                def _():
                    if number == 1 or not both:
                        block(n, list(range(ROWS * PIECES)), first, number, both)
                        return

                    def tiles(tile, inner):
                        pieces = [tile * PIECES + i for i in range(PIECES)]
                        block(n, pieces, first, number, both)
                        return inner

                    lax.fori_loop(0, ROWS, tiles, 0)

        return carry

    lax.fori_loop(0, slots, each, 0)


def call_attend(near, slots, order, windows, rest, near_kv, sides, name):
    devices, _, tokens, _ = rest.shape
    span = devices * tokens
    pairs = slots * span * span * 2
    return pl.pallas_call(
        functools.partial(attend, near, slots, len(sides) > 2),
        out_shape=jax.ShapeDtypeStruct((devices, slots, tokens, HD), jnp.bfloat16),
        in_specs=[SMEM] * 2 + [ANY] * (2 + len(sides)),
        out_specs=VMEM,
        scratch_shapes=[
            pltpu.VMEM((slots, devices, tokens, HD), jnp.bfloat16),
            pltpu.VMEM((slots, 3 * devices, tokens, HD), jnp.bfloat16),
            pltpu.VMEM((slots, 3 * devices, tokens, 2 * HD), jnp.bfloat16),
            pltpu.SemaphoreType.DMA((slots, 7)),
        ],
        compiler_params=pltpu.CompilerParams(vmem_limit_bytes=48 * 2**20),
        cost_estimate=pl.CostEstimate(
            flops=4 * pairs * HD, bytes_accessed=16 * slots * span * HD, transcendentals=pairs
        ),
        name=name,
    )(order, windows, rest, near_kv, *sides)


def shards(queries, keys, values, windows):
    tokens, model = queries.shape
    heads = model // HD
    devices = lax.axis_size("head")
    layers = lax.axis_size("seq")
    slots = heads // devices
    near, far = tuple(range(NEAR)), tuple(range(NEAR, slots))
    windows = windows.T
    steps = 2 if tokens % 32 == 0 else 1
    some = tokens // steps
    rows = pl.BlockSpec((some, model), lambda i: (i, 0))

    def blocks_of(count):
        return pl.BlockSpec((devices, count, some, HD), lambda i: (0, 0, i, 0))

    def packed(blocks):
        return jax.ShapeDtypeStruct((devices, blocks, tokens, HD), jnp.bfloat16)

    def moved(blocks):
        return pl.CostEstimate(
            flops=0, bytes_accessed=4 * devices * blocks * tokens * HD, transcendentals=0
        )

    def swap(array):
        return lax.all_to_all(array, "head", split_axis=0, concat_axis=0, tiled=True)

    def neighbours(array):
        ends = layers - 1
        return (
            lax.ppermute(array, "seq", [(i, i + 1) for i in range(ends)]),
            lax.ppermute(array, "seq", [(i + 1, i) for i in range(ends)]),
        )

    blocks = 2 * len(near)
    first, order = pl.pallas_call(
        functools.partial(pack_first, near),
        grid=(steps,),
        out_shape=(packed(blocks), jax.ShapeDtypeStruct((heads,), jnp.int32)),
        in_specs=[SMEM, rows, rows],
        out_specs=(blocks_of(blocks), SMEM),
        cost_estimate=moved(blocks),
        name="pack_near_keys_values",
    )(windows, keys, values)
    near_kv = swap(first)

    blocks = slots + 2 * len(far)
    second = pl.pallas_call(
        functools.partial(pack_second, tuple(range(slots)), far),
        grid=(steps,),
        out_shape=packed(blocks),
        in_specs=[SMEM, rows, rows, rows],
        out_specs=blocks_of(blocks),
        cost_estimate=moved(blocks),
        name="pack_queries_and_rest",
    )(order, queries, keys, values)
    sides = neighbours(near_kv)
    rest = swap(second)

    def with_far():
        return call_attend(
            NEAR, slots, order, windows, rest, near_kv, (*sides, *neighbours(rest[:, slots:])),
            "attend_all_slots_wide",
        )

    def without_far():
        return call_attend(
            NEAR, slots, order, windows, rest, near_kv, sides, "attend_near_slots_wide"
        )

    wide = jnp.sum(windows[0]) > NEAR * devices
    attended = swap(lax.cond(wide, with_far, without_far))

    return pl.pallas_call(
        unpack,
        grid=(steps,),
        out_shape=jax.ShapeDtypeStruct((tokens, model), jnp.bfloat16),
        in_specs=[SMEM, blocks_of(slots)],
        out_specs=rows,
        cost_estimate=moved(slots),
        name="unpack_attended",
    )(order, attended)


def solution(mesh):
    placed = P(("cfg", "seq", "head"), None)
    return jax.shard_map(
        shards,
        mesh=mesh,
        in_specs=(placed, placed, placed, P()),
        out_specs=placed,
        check_vma=False,
    )
```
